32 devices in a mesh: row: 4 (over y, x), col: 8 (over z, core).
Axes of the slice: x: 2, y: 2, z: 4, core: 2. Of those that a mesh axis runs over, the one named last changes fastest.
Arguments:
- b_gate_up: bfloat16 [512, 28672], P('col', 'row'), may hold values from -6 to 6
- b_down: bfloat16 [256, 28672], P('col', 'row'), may hold values from -6 to 6
- a_gate_up: bfloat16 [512, 28672], P(None, 'row'), may hold values from -6 to 6
- a_down: bfloat16 [256, 28672], P(None, 'row'), may hold values from -6 to 6
- transform: bfloat16 [28672, 28672], P('row', 'col'), may hold values from -0.03125 to 0.03125
- check_tokens: bfloat16 [8192, 256], P('col'), may hold values from -6 to 6
Outputs:
- merged_gate_up: bfloat16 [512, 28672], P(None, 'row')
- merged_down: bfloat16 [256, 28672], P(None, 'row')
- check: bfloat16 [8192, 256], P('col', 'row')
The draws below stay inside these ranges and needn't reach their ends.
All inputs are finite; a program needn't handle non-finite values.
Results may differ from the reference program's by a relative error of at most 0.0081.
Values may be sent and summed in bfloat16 or wider, within the bound.
No kernel may reach another device: no remote copies, remote signals or barrier semaphores. Data moves between devices by JAX's collectives and lax.ppermute only.
A program may use at most 192 MiB of HBM per device.

```python
import jax
import jax.numpy as jnp
from jax import lax

FF = 28672
R = 256
TOK_DEV = 1024
TOKENS = 8192
N_COL = 8


def level_of(own_key, dims, cuts, least, top_value):
    def one(axis_at, shards_of):
        steps = jax.random.uniform(jax.random.fold_in(jax.random.fold_in(own_key, 6), axis_at), (shards_of,), jnp.float32, least / len(cuts), top_value / len(cuts))
        return jnp.repeat(jnp.exp(steps), dims[axis_at] // shards_of).reshape((-1,) + (1,) * (len(dims) - axis_at - 1))

    factor_of = one(*cuts[0])
    for cut in cuts[1:]:
        factor_of = factor_of * one(*cut)
    return factor_of


def centred(stream_key, extent, width, reach, shards=(), dtype=jnp.bfloat16):
    drawn = jax.random.normal(stream_key, extent, jnp.float32) * width
    if len(shards) > 0:
        drawn = level_of(stream_key, extent, shards, -0.22, 0.18) * drawn
    return jnp.clip(drawn, min=-reach, max=reach).astype(dtype)


def setup_inputs(seed: int = 0) -> dict:
    key_of = jax.random.split(jax.random.key(seed), 7)
    b_gate_up = centred(key_of[0], (2 * R, FF), 1.0, 6.0, ((0, 8), (1, 4)))
    b_down = centred(key_of[1], (R, FF), 1.0, 6.0, ((0, 8), (1, 4)))
    a_gate_up = centred(key_of[2], (2 * R, FF), 1.0, 6.0, ((1, 4),))
    a_down = centred(key_of[3], (R, FF), 1.0, 6.0, ((1, 4),))
    transform = centred(key_of[4], (FF, FF), FF ** -0.5, 0.03125, ((0, 4), (1, 8)))
    check_tokens = centred(key_of[5], (TOKENS, R), 1.0, 6.0, ((0, 8),))
    return {"b_gate_up": b_gate_up, "b_down": b_down, "a_gate_up": a_gate_up, "a_down": a_down, "transform": transform, "check_tokens": check_tokens}


def reference(b_gate_up, b_down, a_gate_up, a_down, transform, check_tokens):
    projected_gate_up = jnp.dot(b_gate_up, transform, preferred_element_type=jnp.float32).astype(jnp.bfloat16)
    projected_down = jnp.dot(b_down, transform, preferred_element_type=jnp.float32).astype(jnp.bfloat16)
    merged_gate_up = (0.5 * (a_gate_up.astype(jnp.float32) + projected_gate_up.astype(jnp.float32))).astype(jnp.bfloat16)
    merged_down = (0.5 * (a_down.astype(jnp.float32) + projected_down.astype(jnp.float32))).astype(jnp.bfloat16)
    gate_weight = merged_gate_up[:R]
    up_weight = merged_gate_up[R:]

    def forward(block):
        gate = jnp.dot(block, gate_weight, preferred_element_type=jnp.float32) * (R ** -0.5)
        up = jnp.dot(block, up_weight, preferred_element_type=jnp.float32) * (R ** -0.5)
        hidden = (jax.nn.silu(gate) * up).astype(jnp.bfloat16)
        total = lax.dot_general(hidden, merged_down, (((1,), (1,)), ((), ())), preferred_element_type=jnp.float32)
        return (total * (FF ** -0.5)).astype(jnp.bfloat16)

    blocks = check_tokens.reshape(N_COL, TOK_DEV, R)
    check = lax.map(forward, blocks).reshape(TOKENS, R)
    return merged_gate_up, merged_down, check
```

```python
import functools

import jax
import jax.numpy as jnp
from jax import lax
from jax.experimental import pallas as pl
from jax.experimental.pallas import tpu as pltpu
from jax.sharding import PartitionSpec as P

BF16 = jnp.bfloat16
F32 = jnp.float32
VMEM_BYTES = 48 * 2**20


def ring_order(n):
    return [0, *range(1, n, 2), *reversed(range(2, n, 2))]


def look_up(table, index):
    return sum(jnp.where(index == i, v, 0) for i, v in enumerate(table))


def pick(arrays, index):
    out = arrays[0]
    for i in range(1, len(arrays)):
        out = jnp.where(index == i, arrays[i], out)
    return out


def block_of(width):
    return max(b for b in range(128, 513, 128) if width % b == 0)


def project_kernel(scalars, mine, theirs, panel, out, rows):
    count = mine.shape[0]

    @pl.when(pl.program_id(0) == 0)
    def _():
        rows[:count] = mine[...]
        rows[count:] = theirs[...]

    core = scalars[0]
    product = jnp.dot(rows[...], panel[...], preferred_element_type=F32).astype(BF16)
    out[core] = product[:count]
    out[1 - core] = product[count:]


def project(scalars, mine, theirs, panel):
    count, depth = mine.shape
    width = panel.shape[1]
    block = block_of(width)
    once = pl.Buffered(1)
    return pl.pallas_call(
        project_kernel,
        grid_spec=pltpu.PrefetchScalarGridSpec(
            num_scalar_prefetch=1,
            grid=(width // block,),
            in_specs=[
                pl.BlockSpec((count, depth), lambda i, s: (0, 0), pipeline_mode=once),
                pl.BlockSpec((count, depth), lambda i, s: (0, 0), pipeline_mode=once),
                pl.BlockSpec((depth, block), lambda i, s: (0, i)),
            ],
            out_specs=pl.BlockSpec((2, count, block), lambda i, s: (0, 0, i)),
            scratch_shapes=[pltpu.VMEM((2 * count, depth), BF16)],
        ),
        out_shape=jax.ShapeDtypeStruct((2, count, width), BF16),
        compiler_params=pltpu.CompilerParams(vmem_limit_bytes=VMEM_BYTES),
        name="project",
    )(scalars, mine, theirs, panel).reshape(2 * count, width)


def forward_kernel(steps, groups, scalars, tokens, *refs):
    own, far = refs[:groups], refs[groups : 2 * groups]
    a_gu, a_dn, gu_out, dn_out, check_out, proj, total = refs[2 * groups :]
    step = pl.program_id(0)
    features = tokens.shape[1]
    scale = features ** (-0.5)
    gu_rows = a_gu.shape[0] // (2 * groups)

    def gather(pieces):
        for t in range(groups):
            place = scalars[1 + t]
            proj[2 * place] = pieces[t][: proj.shape[1]]
            proj[2 * place + 1] = pieces[t][proj.shape[1] :]

    @pl.when(step < steps)
    def _():
        gather(own)

    @pl.when(step >= steps)
    def _():
        gather(far)

    proj_gu = proj[:, :gu_rows].reshape(a_gu.shape).astype(F32)
    proj_dn = proj[:, gu_rows:].reshape(a_dn.shape).astype(F32)
    merged_gu = (0.5 * (a_gu[...].astype(F32) + proj_gu)).astype(BF16)
    merged_dn = (0.5 * (a_dn[...].astype(F32) + proj_dn)).astype(BF16)
    gu_out[...] = merged_gu
    dn_out[...] = merged_dn
    gate = jnp.dot(tokens[...], merged_gu[:features], preferred_element_type=F32) * (0.5 * scale)
    up = jnp.dot(tokens[...], merged_gu[features:], preferred_element_type=F32) * scale
    hidden = (gate * (1.0 + jnp.tanh(gate)) * up).astype(BF16)
    part = lax.dot_general(hidden, merged_dn, (((1,), (1,)), ((), ())), preferred_element_type=F32)

    @pl.when(step == 0)
    def _():
        total[...] = part

    @pl.when(step > 0)
    def _():
        total[...] += part

    @pl.when(step == 2 * steps - 1)
    def _():
        width = features // groups
        fold = max(1, 128 // width)
        rows = total.shape[0] // fold
        for j in range(groups):
            packed = [total[f * rows : (f + 1) * rows, j * width : (j + 1) * width] for f in range(fold)]
            check_out[j] = jnp.concatenate(packed, axis=1).astype(BF16)


def forward(scalars, tokens, own, far, a_gu, a_dn):
    groups = len(own)
    piece_rows, width = own[0].shape
    block = block_of(width)
    steps = width // block
    count, features = tokens.shape
    fold = max(1, 128 // (features // groups))
    check_shape = (groups, count // fold, fold * features // groups)

    def own_place(i, s):
        return (0, jnp.minimum(i, steps - 1))

    def far_place(i, s):
        return (0, jnp.maximum(i - steps, 0))

    def place(i, s):
        half = jnp.where(i < steps, s[0], 1 - s[0])
        return (0, half * steps + lax.rem(i, steps))

    gu_spec = pl.BlockSpec((a_gu.shape[0], block), place)
    dn_spec = pl.BlockSpec((a_dn.shape[0], block), place)
    return pl.pallas_call(
        functools.partial(forward_kernel, steps, groups),
        grid_spec=pltpu.PrefetchScalarGridSpec(
            num_scalar_prefetch=1,
            grid=(2 * steps,),
            in_specs=[pl.BlockSpec(tokens.shape, lambda i, s: (0, 0))]
            + [pl.BlockSpec((piece_rows, block), own_place)] * groups
            + [pl.BlockSpec((piece_rows, block), far_place)] * groups
            + [gu_spec, dn_spec],
            out_specs=[gu_spec, dn_spec, pl.BlockSpec(check_shape, lambda i, s: (0, 0, 0))],
            scratch_shapes=[
                pltpu.VMEM((2 * groups, piece_rows // 2, block), BF16),
                pltpu.VMEM((count, features), F32),
            ],
        ),
        out_shape=[
            jax.ShapeDtypeStruct(a_gu.shape, BF16),
            jax.ShapeDtypeStruct(a_dn.shape, BF16),
            jax.ShapeDtypeStruct(check_shape, BF16),
        ],
        compiler_params=pltpu.CompilerParams(vmem_limit_bytes=VMEM_BYTES),
        name="forward",
    )(scalars, tokens, *own, *far, a_gu, a_dn)


def on_device(b_gate_up, b_down, a_gate_up, a_down, transform, check_tokens):
    n = lax.axis_size("row")
    assert lax.axis_size("col") == 2 * n
    q = lax.axis_index("row")
    col = lax.axis_index("col")
    z, core = col // 2, col % 2
    order = ring_order(n)
    place = [order.index(i) for i in range(n)]
    after = {order[i]: order[(i + 1) % n] for i in range(n)}
    ring = [(2 * i + k, 2 * after[i] + k) for i in range(n) for k in range(2)]
    twin = [(i, i ^ 1) for i in range(2 * n)]
    began = [look_up(order, (look_up(place, q) - t) % n) for t in range(n)]
    scalars = jnp.stack([core, *began]).astype(jnp.int32)

    def peers(d):
        return [(i, i ^ d) for i in range(n)]

    width = transform.shape[1]
    rows = jnp.concatenate([b_gate_up, b_down], axis=0)
    part_rows = 2 * rows.shape[0] // n

    def stages(t, rows):
        with jax.named_scope(f"rows_ring_{t}"):
            following = [lax.ppermute(rows, "col", ring)] if t < n - 1 else []
        with jax.named_scope(f"rows_twin_{t}"):
            other = lax.ppermute(rows, "col", twin)
        *_, partial = yield [*following, project(scalars, rows, other, transform)]

        parts = partial.reshape(n, part_rows, width)
        sums = [lax.dynamic_index_in_dim(parts, q, keepdims=False)]
        for d in range(1, n):
            with jax.named_scope(f"reduce_{t}_{d}"):
                part = lax.dynamic_index_in_dim(parts, q ^ d, keepdims=False)
                sums.append(lax.ppermute(part, "row", peers(d)))
        sums = yield sums
        held = [sum(v.astype(F32) for v in sums).astype(BF16)]

        for hop in range(n - 1):
            with jax.named_scope(f"shares_ring_{t}_{hop}"):
                held.append(lax.ppermute(held[-1], "col", ring))
            held = yield held

        def for_row(r):
            return pick(held, (look_up(place, z) - look_up(place, r)) % n)

        got = [for_row(q)]
        for d in range(1, n):
            with jax.named_scope(f"deliver_{t}_{d}"):
                got.append(lax.ppermute(for_row(q ^ d), "row", peers(d)))
        got = yield got

        mine = jnp.concatenate([pick(got, q ^ j) for j in range(n)], axis=0)
        with jax.named_scope(f"deliver_twin_{t}"):
            theirs = lax.ppermute(mine, "col", twin)
        yield [mine, theirs]

    own = [None] * n
    far = [None] * n
    running = {}
    ready = {}
    step = 0
    while step < n or running:
        handed = {t: running[t].send(ready[t]) for t in running}
        if step < n:
            running[step] = stages(step, rows)
            handed[step] = next(running[step])
        flat = lax.optimization_barrier([v for vs in handed.values() for v in vs])
        ready = {}
        for t, vs in handed.items():
            ready[t], flat = flat[: len(vs)], flat[len(vs) :]
        rows = ready[step][0] if step < n else None
        step += 1
        for t in [t for t in ready if step - t == n + 3]:
            own[t], far[t] = ready.pop(t)
            del running[t]

    merged_gate_up, merged_down, parts = forward(scalars, check_tokens, own, far, a_gate_up, a_down)
    total = lax.dynamic_index_in_dim(parts, q, keepdims=False).astype(F32)
    for d in range(1, n):
        with jax.named_scope(f"check_reduce_{d}"):
            sent = lax.dynamic_index_in_dim(parts, q ^ d, keepdims=False)
            total = total + lax.ppermute(sent, "row", peers(d)).astype(F32)
    hidden_units = n * transform.shape[0]
    check = (total * hidden_units ** (-0.5)).astype(BF16)
    count, features = check_tokens.shape
    share = features // n
    check = check.reshape(check.shape[0], -1, share).swapaxes(0, 1).reshape(count, share)
    return merged_gate_up, merged_down, check


def solution(mesh):
    return jax.shard_map(
        on_device,
        mesh=mesh,
        in_specs=(
            P("col", "row"),
            P("col", "row"),
            P(None, "row"),
            P(None, "row"),
            P("row", "col"),
            P("col", None),
        ),
        out_specs=(P(None, "row"), P(None, "row"), P("col", "row")),
        check_vma=False,
    )
```

```python
import functools

import jax
import jax.numpy as jnp
from jax import lax
from jax.experimental import pallas as pl
from jax.experimental.pallas import tpu as pltpu
from jax.sharding import PartitionSpec as P

BF16 = jnp.bfloat16
F32 = jnp.float32
VMEM_BYTES = 48 * 2**20


def ring_order(n):
    return [0, *range(1, n, 2), *reversed(range(2, n, 2))]


def look_up(table, index):
    return sum(jnp.where(index == i, v, 0) for i, v in enumerate(table))


def pick(arrays, index):
    out = arrays[0]
    for i in range(1, len(arrays)):
        out = jnp.where(index == i, arrays[i], out)
    return out


def block_of(width, limit):
    return max(b for b in range(128, limit + 1, 128) if width % b == 0)


def project_kernel(scalars, mine, theirs, panel, out, rows):
    count = mine.shape[0]

    @pl.when(pl.program_id(0) == 0)
    def _():
        rows[:count] = mine[...]
        rows[count:] = theirs[...]

    core = scalars[0]
    product = jnp.dot(rows[...], panel[...], preferred_element_type=F32).astype(BF16)
    out[core] = product[:count]
    out[1 - core] = product[count:]


def project(scalars, mine, theirs, panel):
    count, depth = mine.shape
    width = panel.shape[1]
    block = block_of(width, 512)
    once = pl.Buffered(1)
    return pl.pallas_call(
        project_kernel,
        grid_spec=pltpu.PrefetchScalarGridSpec(
            num_scalar_prefetch=1,
            grid=(width // block,),
            in_specs=[
                pl.BlockSpec((count, depth), lambda i, s: (0, 0), pipeline_mode=once),
                pl.BlockSpec((count, depth), lambda i, s: (0, 0), pipeline_mode=once),
                pl.BlockSpec((depth, block), lambda i, s: (0, i)),
            ],
            out_specs=pl.BlockSpec((2, count, block), lambda i, s: (0, 0, i)),
            scratch_shapes=[pltpu.VMEM((2 * count, depth), BF16)],
        ),
        out_shape=jax.ShapeDtypeStruct((2, count, width), BF16),
        compiler_params=pltpu.CompilerParams(vmem_limit_bytes=VMEM_BYTES),
        name="project",
    )(scalars, mine, theirs, panel).reshape(2 * count, width)


def merge(a, projected):
    return (0.5 * (a.astype(F32) + projected.astype(F32))).astype(BF16)


def merge_kernel(steps, scalars, own, far, a_gu, a_dn, *refs):
    gu_out, dn_out = refs[-2:]
    shard = own.shape[0] // 2
    gu_rows, dn_rows = a_gu.shape[0] // 2, a_dn.shape[0] // 2

    def fill(piece):
        for k in range(2):
            gu, dn = pl.ds(k * gu_rows, gu_rows), pl.ds(k * dn_rows, dn_rows)
            gu_out[gu] = merge(a_gu[gu], piece[pl.ds(k * shard, gu_rows)])
            dn_out[dn] = merge(a_dn[dn], piece[pl.ds(k * shard + gu_rows, dn_rows)])

    @pl.when(pl.program_id(0) < steps)
    def _():
        fill(own)

    @pl.when(pl.program_id(0) >= steps)
    def _():
        fill(far)


def column_specs(width, block, t, groups, piece, a_gu, a_dn):
    steps = width // block
    piece_rows = (a_gu.shape[0] + a_dn.shape[0]) // groups

    def column(i, s):
        return jnp.where(i < steps, s[0], 1 - s[0]) * steps + lax.rem(i, steps)

    own = pl.BlockSpec((piece_rows, block), lambda i, s: (piece, jnp.minimum(i, steps - 1)))
    far = pl.BlockSpec((piece_rows, block), lambda i, s: (piece, jnp.maximum(i - steps, 0)))
    group = [pl.BlockSpec((a.shape[0] // groups, block), lambda i, s: (s[1 + t], column(i, s))) for a in (a_gu, a_dn)]
    slab = [pl.BlockSpec((a.shape[0], block), lambda i, s: (0, column(i, s))) for a in (a_gu, a_dn)]
    return steps, [own, far], group, slab


def merge_group(scalars, t, groups, piece, own, far, a_gu, a_dn, sofar):
    width = own.shape[1]
    block = block_of(width, 2048)
    steps, pieces, group, _ = column_specs(width, block, t, groups, piece, a_gu, a_dn)
    anywhere = [pl.BlockSpec(memory_space=pl.ANY)] * len(sofar)
    return pl.pallas_call(
        functools.partial(merge_kernel, steps),
        grid_spec=pltpu.PrefetchScalarGridSpec(
            num_scalar_prefetch=1, grid=(2 * steps,), in_specs=pieces + group + anywhere, out_specs=group
        ),
        out_shape=[jax.ShapeDtypeStruct(a.shape, BF16) for a in (a_gu, a_dn)],
        input_output_aliases={5 + i: i for i in range(len(sofar))},
        compiler_params=pltpu.CompilerParams(vmem_limit_bytes=VMEM_BYTES),
        name="merge",
    )(scalars, own, far, a_gu, a_dn, *sofar)


def forward_kernel(steps, groups, t, scalars, tokens, own, far, a_gu, a_dn, gu, dn, gu_out, dn_out, check_out, gu_all, dn_all, total):
    step = pl.program_id(0)
    features = tokens.shape[1]
    scale = features ** (-0.5)
    merge_kernel(steps, scalars, own, far, a_gu, a_dn, gu_out, dn_out)
    for whole, before, part in ((gu_all, gu, gu_out), (dn_all, dn, dn_out)):
        whole[...] = before[...]
        rows = part.shape[0]
        whole[pl.ds(pl.multiple_of(scalars[1 + t] * rows, rows), rows)] = part[...]
    block = gu.shape[1]
    chunk = block_of(block, 256)
    part = 0.0
    for start in range(0, block, chunk):
        columns = slice(start, start + chunk)
        gate = jnp.dot(tokens[...], gu_all[:features, columns], preferred_element_type=F32) * (0.5 * scale)
        up = jnp.dot(tokens[...], gu_all[features:, columns], preferred_element_type=F32) * scale
        hidden = (gate * (1.0 + jnp.tanh(gate)) * up).astype(BF16)
        part += lax.dot_general(hidden, dn_all[:, columns], (((1,), (1,)), ((), ())), preferred_element_type=F32)

    @pl.when(step == 0)
    def _():
        total[...] = part

    @pl.when(step > 0)
    def _():
        total[...] += part

    @pl.when(step == 2 * steps - 1)
    def _():
        width = features // groups
        fold = max(1, 128 // width)
        rows = total.shape[0] // fold
        for j in range(groups):
            packed = [total[f * rows : (f + 1) * rows, j * width : (j + 1) * width] for f in range(fold)]
            check_out[j] = jnp.concatenate(packed, axis=1).astype(BF16)


def forward(scalars, tokens, t, groups, own, far, a_gu, a_dn, sofar):
    width = own.shape[1]
    block = block_of(width, 2048)
    count, features = tokens.shape
    fold = max(1, 128 // (features // groups))
    check_shape = (groups, count // fold, fold * features // groups)
    steps, pieces, group, slab = column_specs(width, block, t, groups, 0, a_gu, a_dn)
    return pl.pallas_call(
        functools.partial(forward_kernel, steps, groups, t),
        grid_spec=pltpu.PrefetchScalarGridSpec(
            num_scalar_prefetch=1,
            grid=(2 * steps,),
            in_specs=[pl.BlockSpec(tokens.shape, lambda i, s: (0, 0))] + pieces + group + slab,
            out_specs=group + [pl.BlockSpec(check_shape, lambda i, s: (0, 0, 0))],
            scratch_shapes=[
                pltpu.VMEM((a_gu.shape[0], block), BF16),
                pltpu.VMEM((a_dn.shape[0], block), BF16),
                pltpu.VMEM((count, features), F32),
            ],
        ),
        out_shape=[
            jax.ShapeDtypeStruct(a_gu.shape, BF16),
            jax.ShapeDtypeStruct(a_dn.shape, BF16),
            jax.ShapeDtypeStruct(check_shape, BF16),
        ],
        input_output_aliases={6: 0, 7: 1},
        compiler_params=pltpu.CompilerParams(vmem_limit_bytes=VMEM_BYTES),
        name="forward",
    )(scalars, tokens, own, far, a_gu, a_dn, *sofar)


def on_device(b_gate_up, b_down, a_gate_up, a_down, transform, check_tokens):
    n = lax.axis_size("row")
    assert lax.axis_size("col") == 2 * n
    q = lax.axis_index("row")
    col = lax.axis_index("col")
    z, core = col // 2, col % 2
    order = ring_order(n)
    place = [order.index(i) for i in range(n)]
    after = {order[i]: order[(i + 1) % n] for i in range(n)}
    ring = [(2 * i + k, 2 * after[i] + k) for i in range(n) for k in range(2)]
    back = [(j, i) for i, j in ring]
    twin = [(i, i ^ 1) for i in range(2 * n)]
    began = [look_up(order, (look_up(place, q) - t) % n) for t in range(n)]
    scalars = jnp.stack([core, *began]).astype(jnp.int32)

    def peers(d):
        return [(i, i ^ d) for i in range(n)]

    width = transform.shape[1]
    rows = jnp.concatenate([b_gate_up, b_down], axis=0)
    part_rows = 2 * rows.shape[0] // n

    def cat(arrays):
        return arrays[0] if len(arrays) == 1 else jnp.concatenate(arrays, axis=0)

    def along_ring(perm, name, held, step):
        if not step:
            return None
        with jax.named_scope(name):
            return lax.ppermute(cat([held[t][i] for t, i, _ in step]), "col", perm)

    def split(arrived, held, step):
        for i, (t, _, to) in enumerate(step):
            held[t][to] = arrived[i * part_rows : (i + 1) * part_rows]

    def for_row(held, r):
        return pick([held[i] for i in range(n)], (look_up(place, r) - look_up(place, z)) % n)

    half = n // 2
    partial, sums, held, got = {}, {}, {}, {}
    sofar = []
    for step in range(n + half + 3):
        out = {}
        if step < n:
            if step < n - 1:
                with jax.named_scope(f"rows_ring_{step}"):
                    out["rows"] = lax.ppermute(rows, "col", ring)
            with jax.named_scope(f"rows_twin_{step}"):
                other = lax.ppermute(rows, "col", twin)
            out["partial"] = project(scalars, rows, other, transform)
        if 0 <= step - 1 < n:
            parts = partial[step - 1].reshape(n, part_rows, width)
            out["sums"] = [lax.dynamic_index_in_dim(parts, q, keepdims=False)]
            for d in range(1, n):
                with jax.named_scope(f"reduce_{step - 1}_{d}"):
                    part = lax.dynamic_index_in_dim(parts, q ^ d, keepdims=False)
                    out["sums"].append(lax.ppermute(part, "row", peers(d)))
        if 0 <= step - 2 < n:
            held[step - 2] = {0: sum(v.astype(F32) for v in sums[step - 2]).astype(BF16)}
        onward, backward = [], []
        for t in range(n):
            hop = step - 2 - t
            if 0 <= hop < half:
                onward.append((t, hop, hop + 1))
                if hop:
                    backward.append((t, (1 - hop) % n, n - hop))
        out["onward"] = along_ring(back, f"shares_onward_{step}", held, onward)
        out["backward"] = along_ring(ring, f"shares_backward_{step}", held, backward)
        deliver = [t for t in range(n) if step == max(t + 2 + half, n + 1)]
        if deliver:
            out["got"] = [cat([for_row(held[t], q) for t in deliver])]
            for d in range(1, n):
                with jax.named_scope(f"deliver_{step}_{d}"):
                    out["got"].append(lax.ppermute(cat([for_row(held[t], q ^ d) for t in deliver]), "row", peers(d)))
        if got:
            arrived = got.pop(step - 1)
            count = arrived[0].shape[0] // part_rows
            pieces = []
            for i in range(count):
                own = [v[i * part_rows : (i + 1) * part_rows] for v in arrived]
                pieces += [pick(own, q ^ j) for j in range(n)]
            own = cat(pieces)
            with jax.named_scope(f"deliver_twin_{step}"):
                far = lax.ppermute(own, "col", twin)
            for i, t in enumerate(delivered):
                if t < n - 1:
                    sofar = merge_group(scalars, t, n, i, own, far, a_gate_up, a_down, sofar)
        out["sofar"] = sofar

        leaves, tree = jax.tree.flatten(out)
        out = jax.tree.unflatten(tree, lax.optimization_barrier(leaves))
        rows = out.get("rows")
        if "partial" in out:
            partial[step] = out["partial"]
        if "sums" in out:
            sums[step - 1] = out["sums"]
        split(out["onward"], held, onward)
        split(out["backward"], held, backward)
        if "got" in out:
            got[step] = out["got"]
            delivered = deliver
        sofar = out["sofar"]

    merged_gate_up, merged_down, parts = forward(
        scalars, check_tokens, n - 1, n, own, far, a_gate_up, a_down, sofar
    )
    total = lax.dynamic_index_in_dim(parts, q, keepdims=False).astype(F32)
    for d in range(1, n):
        with jax.named_scope(f"check_reduce_{d}"):
            sent = lax.dynamic_index_in_dim(parts, q ^ d, keepdims=False)
            total = total + lax.ppermute(sent, "row", peers(d)).astype(F32)
    hidden_units = n * transform.shape[0]
    check = (total * hidden_units ** (-0.5)).astype(BF16)
    count, features = check_tokens.shape
    share = features // n
    check = check.reshape(check.shape[0], -1, share).swapaxes(0, 1).reshape(count, share)
    return merged_gate_up, merged_down, check


def solution(mesh):
    return jax.shard_map(
        on_device,
        mesh=mesh,
        in_specs=(
            P("col", "row"),
            P("col", "row"),
            P(None, "row"),
            P(None, "row"),
            P("row", "col"),
            P("col", None),
        ),
        out_specs=(P(None, "row"), P(None, "row"), P("col", "row")),
        check_vma=False,
    )
```

```python
import functools

import jax
import jax.numpy as jnp
from jax import lax
from jax.experimental import pallas as pl
from jax.experimental.pallas import tpu as pltpu
from jax.sharding import PartitionSpec as P

BF16 = jnp.bfloat16
F32 = jnp.float32
VMEM_BYTES = 48 * 2**20


def ring_order(n):
    return [0, *range(1, n, 2), *reversed(range(2, n, 2))]


def look_up(table, index):
    return sum(jnp.where(index == i, v, 0) for i, v in enumerate(table))


def pick(arrays, index):
    out = arrays[0]
    for i in range(1, len(arrays)):
        out = jnp.where(index == i, arrays[i], out)
    return out


def block_of(width, limit):
    return max(b for b in range(128, limit + 1, 128) if width % b == 0)


def project_kernel(scalars, mine, theirs, panel, out, rows):
    count = mine.shape[0]

    @pl.when(pl.program_id(0) == 0)
    def _():
        rows[:count] = mine[...]
        rows[count:] = theirs[...]

    core = scalars[0]
    product = jnp.dot(rows[...], panel[...], preferred_element_type=F32).astype(BF16)
    out[core] = product[:count]
    out[1 - core] = product[count:]


def project(scalars, mine, theirs, panel):
    count, depth = mine.shape
    width = panel.shape[1]
    block = block_of(width, 512)
    once = pl.Buffered(1)
    return pl.pallas_call(
        project_kernel,
        grid_spec=pltpu.PrefetchScalarGridSpec(
            num_scalar_prefetch=1,
            grid=(width // block,),
            in_specs=[
                pl.BlockSpec((count, depth), lambda i, s: (0, 0), pipeline_mode=once),
                pl.BlockSpec((count, depth), lambda i, s: (0, 0), pipeline_mode=once),
                pl.BlockSpec((depth, block), lambda i, s: (0, i)),
            ],
            out_specs=pl.BlockSpec((2, count, block), lambda i, s: (0, 0, i)),
            scratch_shapes=[pltpu.VMEM((2 * count, depth), BF16)],
        ),
        out_shape=jax.ShapeDtypeStruct((2, count, width), BF16),
        compiler_params=pltpu.CompilerParams(vmem_limit_bytes=VMEM_BYTES),
        name="project",
    )(scalars, mine, theirs, panel).reshape(2 * count, width)


def merge(a, projected):
    return (0.5 * (a.astype(F32) + projected.astype(F32))).astype(BF16)


def merge_kernel(steps, scalars, own, far, a_gu, a_dn, *refs):
    gu_out, dn_out = refs[-2:]
    shard = own.shape[0] // 2
    gu_rows, dn_rows = a_gu.shape[0] // 2, a_dn.shape[0] // 2

    def fill(piece):
        for k in range(2):
            gu, dn = pl.ds(k * gu_rows, gu_rows), pl.ds(k * dn_rows, dn_rows)
            gu_out[gu] = merge(a_gu[gu], piece[pl.ds(k * shard, gu_rows)])
            dn_out[dn] = merge(a_dn[dn], piece[pl.ds(k * shard + gu_rows, dn_rows)])

    @pl.when(pl.program_id(0) < steps)
    def _():
        fill(own)

    @pl.when(pl.program_id(0) >= steps)
    def _():
        fill(far)


def column_specs(width, block, t, groups, piece, a_gu, a_dn):
    steps = width // block
    piece_rows = (a_gu.shape[0] + a_dn.shape[0]) // groups

    def column(i, s):
        return jnp.where(i < steps, s[0], 1 - s[0]) * steps + lax.rem(i, steps)

    own = pl.BlockSpec((piece_rows, block), lambda i, s: (piece, jnp.minimum(i, steps - 1)))
    far = pl.BlockSpec((piece_rows, block), lambda i, s: (piece, jnp.maximum(i - steps, 0)))
    group = [pl.BlockSpec((a.shape[0] // groups, block), lambda i, s: (s[1 + t], column(i, s))) for a in (a_gu, a_dn)]
    slab = [pl.BlockSpec((a.shape[0], block), lambda i, s: (0, column(i, s))) for a in (a_gu, a_dn)]
    return steps, [own, far], group, slab


def merge_group(scalars, t, groups, piece, own, far, a_gu, a_dn, sofar):
    width = own.shape[1]
    block = block_of(width, 2048)
    steps, pieces, group, _ = column_specs(width, block, t, groups, piece, a_gu, a_dn)
    anywhere = [pl.BlockSpec(memory_space=pl.ANY)] * len(sofar)
    return pl.pallas_call(
        functools.partial(merge_kernel, steps),
        grid_spec=pltpu.PrefetchScalarGridSpec(
            num_scalar_prefetch=1, grid=(2 * steps,), in_specs=pieces + group + anywhere, out_specs=group
        ),
        out_shape=[jax.ShapeDtypeStruct(a.shape, BF16) for a in (a_gu, a_dn)],
        input_output_aliases={5 + i: i for i in range(len(sofar))},
        compiler_params=pltpu.CompilerParams(vmem_limit_bytes=VMEM_BYTES),
        name="merge",
    )(scalars, own, far, a_gu, a_dn, *sofar)


def ready_kernel(scalars, tokens, rows, out):
    out[...] = jnp.dot(tokens[...], rows[...], preferred_element_type=F32).astype(BF16)


def gate_is_ready(scalars, t, groups):
    return scalars[1 + t] >= groups // 2


def ready_half(scalars, tokens, t, groups, gu):
    count, features = tokens.shape
    block = block_of(gu.shape[1], 2048)
    return pl.pallas_call(
        ready_kernel,
        grid_spec=pltpu.PrefetchScalarGridSpec(
            num_scalar_prefetch=1,
            grid=(gu.shape[1] // block,),
            in_specs=[
                pl.BlockSpec(tokens.shape, lambda i, s: (0, 0)),
                pl.BlockSpec((features, block), lambda i, s: (jnp.where(gate_is_ready(s, t, groups), 0, 1), i)),
            ],
            out_specs=pl.BlockSpec((count, block), lambda i, s: (0, i)),
        ),
        out_shape=jax.ShapeDtypeStruct((count, gu.shape[1]), BF16),
        compiler_params=pltpu.CompilerParams(vmem_limit_bytes=VMEM_BYTES),
        name="ready",
    )(scalars, tokens, gu)


def forward_kernel(steps, groups, t, scalars, tokens, own, far, a_gu, a_dn, ready, gu, dn, gu_out, dn_out, check_out, total, hidden):
    step = pl.program_id(0)
    features = tokens.shape[1]
    scale = features ** (-0.5)
    merge_kernel(steps, scalars, own, far, a_gu, a_dn, gu_out, dn_out)
    place = scalars[1 + t]
    gate_ready = gate_is_ready(scalars, t, groups)
    block = gu.shape[1]
    chunk = block_of(block, 256)

    def with_last(others, part, place, columns):
        rows = part.shape[0]
        pieces = [others[i * rows : (i + 1) * rows, columns] for i in range(others.shape[0] // rows)]
        return jnp.concatenate([jnp.where(place == i, part[:, columns], v) for i, v in enumerate(pieces)], axis=0)

    def run(gate_ready):
        part = 0.0
        for start in range(0, block, chunk):
            columns = slice(start, start + chunk)
            rows = with_last(gu, gu_out, place - groups // 2 if gate_ready else place, columns)
            found = jnp.dot(tokens[...], rows, preferred_element_type=F32)
            known = ready[:, columns].astype(F32)
            gate, up = (known, found) if gate_ready else (found, known)
            gate = gate * (0.5 * scale)
            value = (gate * (1.0 + jnp.tanh(gate)) * (up * scale)).astype(BF16)
            part += lax.dot_general(
                value, with_last(dn, dn_out, place, columns), (((1,), (1,)), ((), ())), preferred_element_type=F32
            )
        hidden[...] = part

    @pl.when(gate_ready)
    def _():
        run(True)

    @pl.when(jnp.logical_not(gate_ready))
    def _():
        run(False)

    @pl.when(step == 0)
    def _():
        total[...] = hidden[...]

    @pl.when(step > 0)
    def _():
        total[...] += hidden[...]

    @pl.when(step == 2 * steps - 1)
    def _():
        width = features // groups
        fold = max(1, 128 // width)
        rows = total.shape[0] // fold
        for j in range(groups):
            packed = [total[f * rows : (f + 1) * rows, j * width : (j + 1) * width] for f in range(fold)]
            check_out[j] = jnp.concatenate(packed, axis=1).astype(BF16)


def forward(scalars, tokens, t, groups, own, far, a_gu, a_dn, ready, sofar):
    width = own.shape[1]
    block = block_of(width, 2048)
    count, features = tokens.shape
    fold = max(1, 128 // (features // groups))
    check_shape = (groups, count // fold, fold * features // groups)
    steps, pieces, group, slab = column_specs(width, block, t, groups, 0, a_gu, a_dn)

    def column(i, s):
        return jnp.where(i < steps, s[0], 1 - s[0]) * steps + lax.rem(i, steps)

    half = pl.BlockSpec(
        (features, block), lambda i, s: (jnp.where(gate_is_ready(s, t, groups), 1, 0), column(i, s))
    )
    known = pl.BlockSpec((count, block), lambda i, s: (0, column(i, s)))
    return pl.pallas_call(
        functools.partial(forward_kernel, steps, groups, t),
        grid_spec=pltpu.PrefetchScalarGridSpec(
            num_scalar_prefetch=1,
            grid=(2 * steps,),
            in_specs=[pl.BlockSpec(tokens.shape, lambda i, s: (0, 0))] + pieces + group + [known, half, slab[1]],
            out_specs=group + [pl.BlockSpec(check_shape, lambda i, s: (0, 0, 0))],
            scratch_shapes=[pltpu.VMEM((count, features), F32), pltpu.VMEM((count, features), F32)],
        ),
        out_shape=[
            jax.ShapeDtypeStruct(a_gu.shape, BF16),
            jax.ShapeDtypeStruct(a_dn.shape, BF16),
            jax.ShapeDtypeStruct(check_shape, BF16),
        ],
        input_output_aliases={7: 0, 8: 1},
        compiler_params=pltpu.CompilerParams(vmem_limit_bytes=VMEM_BYTES),
        name="forward",
    )(scalars, tokens, own, far, a_gu, a_dn, ready, *sofar)


def on_device(b_gate_up, b_down, a_gate_up, a_down, transform, check_tokens):
    n = lax.axis_size("row")
    assert lax.axis_size("col") == 2 * n
    q = lax.axis_index("row")
    col = lax.axis_index("col")
    z, core = col // 2, col % 2
    order = ring_order(n)
    place = [order.index(i) for i in range(n)]
    after = {order[i]: order[(i + 1) % n] for i in range(n)}
    ring = [(2 * i + k, 2 * after[i] + k) for i in range(n) for k in range(2)]
    back = [(j, i) for i, j in ring]
    twin = [(i, i ^ 1) for i in range(2 * n)]
    began = [look_up(order, (look_up(place, q) - t) % n) for t in range(n)]
    scalars = jnp.stack([core, *began]).astype(jnp.int32)

    def peers(d):
        return [(i, i ^ d) for i in range(n)]

    width = transform.shape[1]
    rows = jnp.concatenate([b_gate_up, b_down], axis=0)
    part_rows = 2 * rows.shape[0] // n

    def cat(arrays):
        return arrays[0] if len(arrays) == 1 else jnp.concatenate(arrays, axis=0)

    def along_ring(perm, name, held, step):
        if not step:
            return None
        with jax.named_scope(name):
            return lax.ppermute(cat([held[t][i] for t, i, _ in step]), "col", perm)

    def split(arrived, held, step):
        for i, (t, _, to) in enumerate(step):
            held[t][to] = arrived[i * part_rows : (i + 1) * part_rows]

    def for_row(held, r):
        return pick([held[i] for i in range(n)], (look_up(place, r) - look_up(place, z)) % n)

    half = n // 2
    partial, sums, held, got = {}, {}, {}, {}
    sofar, ready = [], None
    for step in range(n + half + 3):
        out = {}
        if step < n:
            if step < n - 1:
                with jax.named_scope(f"rows_ring_{step}"):
                    out["rows"] = lax.ppermute(rows, "col", ring)
            with jax.named_scope(f"rows_twin_{step}"):
                other = lax.ppermute(rows, "col", twin)
            out["partial"] = project(scalars, rows, other, transform)
        if 0 <= step - 1 < n:
            parts = partial[step - 1].reshape(n, part_rows, width)
            out["sums"] = [lax.dynamic_index_in_dim(parts, q, keepdims=False)]
            for d in range(1, n):
                with jax.named_scope(f"reduce_{step - 1}_{d}"):
                    part = lax.dynamic_index_in_dim(parts, q ^ d, keepdims=False)
                    out["sums"].append(lax.ppermute(part, "row", peers(d)))
        if 0 <= step - 2 < n:
            held[step - 2] = {0: sum(v.astype(F32) for v in sums[step - 2]).astype(BF16)}
        onward, backward = [], []
        for t in range(n):
            hop = step - 2 - t
            if 0 <= hop < half:
                onward.append((t, hop, hop + 1))
                if t == n - 1:
                    if hop + 1 < half:
                        backward.append((t, -hop % n, n - hop - 1))
                elif hop:
                    backward.append((t, (1 - hop) % n, n - hop))
        out["onward"] = along_ring(back, f"shares_onward_{step}", held, onward)
        out["backward"] = along_ring(ring, f"shares_backward_{step}", held, backward)
        deliver = [t for t in range(n) if step == max(t + 2 + half, n + 1)]
        if deliver:
            out["got"] = [cat([for_row(held[t], q) for t in deliver])]
            for d in range(1, n):
                with jax.named_scope(f"deliver_{step}_{d}"):
                    out["got"].append(lax.ppermute(cat([for_row(held[t], q ^ d) for t in deliver]), "row", peers(d)))
        if got:
            arrived = got.pop(step - 1)
            count = arrived[0].shape[0] // part_rows
            pieces = []
            for i in range(count):
                own = [v[i * part_rows : (i + 1) * part_rows] for v in arrived]
                pieces += [pick(own, q ^ j) for j in range(n)]
            own = cat(pieces)
            with jax.named_scope(f"deliver_twin_{step}"):
                far = lax.ppermute(own, "col", twin)
            for i, t in enumerate(delivered):
                if t < n - 1:
                    sofar = merge_group(scalars, t, n, i, own, far, a_gate_up, a_down, sofar)
            if n - 1 not in delivered:
                ready = ready_half(scalars, check_tokens, n - 1, n, sofar[0]) if n - 2 in delivered else None
        out["sofar"] = sofar
        out["ready"] = ready

        leaves, tree = jax.tree.flatten(out)
        out = jax.tree.unflatten(tree, lax.optimization_barrier(leaves))
        rows = out.get("rows")
        if "partial" in out:
            partial[step] = out["partial"]
        if "sums" in out:
            sums[step - 1] = out["sums"]
        split(out["onward"], held, onward)
        split(out["backward"], held, backward)
        if "got" in out:
            got[step] = out["got"]
            delivered = deliver
        sofar, ready = out["sofar"], out["ready"]

    merged_gate_up, merged_down, parts = forward(
        scalars, check_tokens, n - 1, n, own, far, a_gate_up, a_down, ready, sofar
    )
    total = lax.dynamic_index_in_dim(parts, q, keepdims=False).astype(F32)
    for d in range(1, n):
        with jax.named_scope(f"check_reduce_{d}"):
            sent = lax.dynamic_index_in_dim(parts, q ^ d, keepdims=False)
            total = total + lax.ppermute(sent, "row", peers(d)).astype(F32)
    hidden_units = n * transform.shape[0]
    check = (total * hidden_units ** (-0.5)).astype(BF16)
    count, features = check_tokens.shape
    share = features // n
    check = check.reshape(check.shape[0], -1, share).swapaxes(0, 1).reshape(count, share)
    return merged_gate_up, merged_down, check


def solution(mesh):
    return jax.shard_map(
        on_device,
        mesh=mesh,
        in_specs=(
            P("col", "row"),
            P("col", "row"),
            P(None, "row"),
            P(None, "row"),
            P("row", "col"),
            P("col", None),
        ),
        out_specs=(P(None, "row"), P(None, "row"), P("col", "row")),
        check_vma=False,
    )
```

```python
import functools

import jax
import jax.numpy as jnp
from jax import lax
from jax.experimental import pallas as pl
from jax.experimental.pallas import tpu as pltpu
from jax.sharding import PartitionSpec as P

BF16 = jnp.bfloat16
F32 = jnp.float32
VMEM_BYTES = 48 * 2**20


def ring_order(n):
    return [0, *range(1, n, 2), *reversed(range(2, n, 2))]


def look_up(table, index):
    return sum(jnp.where(index == i, v, 0) for i, v in enumerate(table))


def pick(arrays, index):
    out = arrays[0]
    for i in range(1, len(arrays)):
        out = jnp.where(index == i, arrays[i], out)
    return out


def block_of(width, limit):
    return max(b for b in range(128, limit + 1, 128) if width % b == 0)


def project_kernel(scalars, mine, theirs, panel, out, rows):
    count = mine.shape[0]

    @pl.when(pl.program_id(0) == 0)
    def _():
        rows[:count] = mine[...]
        rows[count:] = theirs[...]

    core = scalars[0]
    product = jnp.dot(rows[...], panel[...], preferred_element_type=F32).astype(BF16)
    out[core] = product[:count]
    out[1 - core] = product[count:]


def project(scalars, mine, theirs, panel):
    count, depth = mine.shape
    width = panel.shape[1]
    block = block_of(width, 512)
    once = pl.Buffered(1)
    return pl.pallas_call(
        project_kernel,
        grid_spec=pltpu.PrefetchScalarGridSpec(
            num_scalar_prefetch=1,
            grid=(width // block,),
            in_specs=[
                pl.BlockSpec((count, depth), lambda i, s: (0, 0), pipeline_mode=once),
                pl.BlockSpec((count, depth), lambda i, s: (0, 0), pipeline_mode=once),
                pl.BlockSpec((depth, block), lambda i, s: (0, i)),
            ],
            out_specs=pl.BlockSpec((2, count, block), lambda i, s: (0, 0, i)),
            scratch_shapes=[pltpu.VMEM((2 * count, depth), BF16)],
        ),
        out_shape=jax.ShapeDtypeStruct((2, count, width), BF16),
        compiler_params=pltpu.CompilerParams(vmem_limit_bytes=VMEM_BYTES),
        name="project",
    )(scalars, mine, theirs, panel).reshape(2 * count, width)


def merge(a, projected):
    return (0.5 * (a.astype(F32) + projected.astype(F32))).astype(BF16)


def merge_kernel(steps, scalars, own, far, a_gu, a_dn, *refs):
    gu_out, dn_out = refs[-2:]
    shard = own.shape[0] // 2
    gu_rows, dn_rows = a_gu.shape[0] // 2, a_dn.shape[0] // 2

    def fill(piece):
        for k in range(2):
            gu, dn = pl.ds(k * gu_rows, gu_rows), pl.ds(k * dn_rows, dn_rows)
            gu_out[gu] = merge(a_gu[gu], piece[pl.ds(k * shard, gu_rows)])
            dn_out[dn] = merge(a_dn[dn], piece[pl.ds(k * shard + gu_rows, dn_rows)])

    @pl.when(pl.program_id(0) < steps)
    def _():
        fill(own)

    @pl.when(pl.program_id(0) >= steps)
    def _():
        fill(far)


def column_specs(width, block, t, groups, piece, a_gu, a_dn):
    steps = width // block
    piece_rows = (a_gu.shape[0] + a_dn.shape[0]) // groups

    def column(i, s):
        return jnp.where(i < steps, s[0], 1 - s[0]) * steps + lax.rem(i, steps)

    own = pl.BlockSpec((piece_rows, block), lambda i, s: (piece, jnp.minimum(i, steps - 1)))
    far = pl.BlockSpec((piece_rows, block), lambda i, s: (piece, jnp.maximum(i - steps, 0)))
    group = [pl.BlockSpec((a.shape[0] // groups, block), lambda i, s: (s[1 + t], column(i, s))) for a in (a_gu, a_dn)]
    slab = [pl.BlockSpec((a.shape[0], block), lambda i, s: (0, column(i, s))) for a in (a_gu, a_dn)]
    return steps, [own, far], group, slab


def merge_group(scalars, t, groups, piece, own, far, a_gu, a_dn, sofar):
    width = own.shape[1]
    block = block_of(width, 2048)
    steps, pieces, group, _ = column_specs(width, block, t, groups, piece, a_gu, a_dn)
    anywhere = [pl.BlockSpec(memory_space=pl.ANY)] * len(sofar)
    return pl.pallas_call(
        functools.partial(merge_kernel, steps),
        grid_spec=pltpu.PrefetchScalarGridSpec(
            num_scalar_prefetch=1, grid=(2 * steps,), in_specs=pieces + group + anywhere, out_specs=group
        ),
        out_shape=[jax.ShapeDtypeStruct(a.shape, BF16) for a in (a_gu, a_dn)],
        input_output_aliases={5 + i: i for i in range(len(sofar))},
        compiler_params=pltpu.CompilerParams(vmem_limit_bytes=VMEM_BYTES),
        name="merge",
    )(scalars, own, far, a_gu, a_dn, *sofar)


def ready_kernel(scalars, tokens, rows, out):
    out[...] = jnp.dot(tokens[...], rows[...], preferred_element_type=F32).astype(BF16)


def gate_is_ready(scalars, t, groups):
    return scalars[1 + t] >= groups // 2


def ready_half(scalars, tokens, t, groups, gu):
    count, features = tokens.shape
    block = block_of(gu.shape[1], 2048)
    return pl.pallas_call(
        ready_kernel,
        grid_spec=pltpu.PrefetchScalarGridSpec(
            num_scalar_prefetch=1,
            grid=(gu.shape[1] // block,),
            in_specs=[
                pl.BlockSpec(tokens.shape, lambda i, s: (0, 0)),
                pl.BlockSpec((features, block), lambda i, s: (jnp.where(gate_is_ready(s, t, groups), 0, 1), i)),
            ],
            out_specs=pl.BlockSpec((count, block), lambda i, s: (0, i)),
        ),
        out_shape=jax.ShapeDtypeStruct((count, gu.shape[1]), BF16),
        compiler_params=pltpu.CompilerParams(vmem_limit_bytes=VMEM_BYTES),
        name="ready",
    )(scalars, tokens, gu)


def forward_kernel(steps, groups, t, scalars, tokens, own, far, a_gu, a_dn, ready, gu, dn, gu_out, dn_out, check_out, total):
    step = pl.program_id(0)
    features = tokens.shape[1]
    scale = features ** (-0.5)
    merge_kernel(steps, scalars, own, far, a_gu, a_dn, gu_out, dn_out)
    place = scalars[1 + t]
    gate_ready = gate_is_ready(scalars, t, groups)
    block = gu.shape[1]
    chunk = block_of(block, 256)

    def with_last(others, part, place, columns):
        rows = part.shape[0]
        pieces = [others[i * rows : (i + 1) * rows, columns] for i in range(others.shape[0] // rows)]
        return jnp.concatenate([jnp.where(place == i, part[:, columns], v) for i, v in enumerate(pieces)], axis=0)

    def run(gate_ready):
        part = 0.0
        for start in range(0, block, chunk):
            columns = slice(start, start + chunk)
            rows = with_last(gu, gu_out, place - groups // 2 if gate_ready else place, columns)
            found = jnp.dot(tokens[...], rows, preferred_element_type=F32)
            known = ready[:, columns].astype(F32)
            gate, up = (known, found) if gate_ready else (found, known)
            gate = gate * (0.5 * scale)
            value = (gate * (1.0 + jnp.tanh(gate)) * (up * scale)).astype(BF16)
            part += lax.dot_general(
                value, with_last(dn, dn_out, place, columns), (((1,), (1,)), ((), ())), preferred_element_type=F32
            )
        total[...] += part

    @pl.when(step == 0)
    def _():
        total[...] = jnp.zeros_like(total)

    @pl.when(gate_ready)
    def _():
        run(True)

    @pl.when(jnp.logical_not(gate_ready))
    def _():
        run(False)

    @pl.when(step == 2 * steps - 1)
    def _():
        width = features // groups
        fold = max(1, 128 // width)
        rows = total.shape[0] // fold
        for j in range(groups):
            packed = [total[f * rows : (f + 1) * rows, j * width : (j + 1) * width] for f in range(fold)]
            check_out[j] = jnp.concatenate(packed, axis=1).astype(BF16)


def forward(scalars, tokens, t, groups, own, far, a_gu, a_dn, ready, sofar):
    width = own.shape[1]
    block = block_of(width, 2048)
    count, features = tokens.shape
    fold = max(1, 128 // (features // groups))
    check_shape = (groups, count // fold, fold * features // groups)
    steps, pieces, group, slab = column_specs(width, block, t, groups, 0, a_gu, a_dn)

    def column(i, s):
        return jnp.where(i < steps, s[0], 1 - s[0]) * steps + lax.rem(i, steps)

    half = pl.BlockSpec(
        (features, block), lambda i, s: (jnp.where(gate_is_ready(s, t, groups), 1, 0), column(i, s))
    )
    known = pl.BlockSpec((count, block), lambda i, s: (0, column(i, s)))
    return pl.pallas_call(
        functools.partial(forward_kernel, steps, groups, t),
        grid_spec=pltpu.PrefetchScalarGridSpec(
            num_scalar_prefetch=1,
            grid=(2 * steps,),
            in_specs=[pl.BlockSpec(tokens.shape, lambda i, s: (0, 0))] + pieces + group + [known, half, slab[1]],
            out_specs=group + [pl.BlockSpec(check_shape, lambda i, s: (0, 0, 0))],
            scratch_shapes=[pltpu.VMEM((count, features), F32)],
        ),
        out_shape=[
            jax.ShapeDtypeStruct(a_gu.shape, BF16),
            jax.ShapeDtypeStruct(a_dn.shape, BF16),
            jax.ShapeDtypeStruct(check_shape, BF16),
        ],
        input_output_aliases={7: 0, 8: 1},
        compiler_params=pltpu.CompilerParams(vmem_limit_bytes=VMEM_BYTES),
        name="forward",
    )(scalars, tokens, own, far, a_gu, a_dn, ready, *sofar)


def on_device(b_gate_up, b_down, a_gate_up, a_down, transform, check_tokens):
    n = lax.axis_size("row")
    assert lax.axis_size("col") == 2 * n
    q = lax.axis_index("row")
    col = lax.axis_index("col")
    z, core = col // 2, col % 2
    order = ring_order(n)
    place = [order.index(i) for i in range(n)]
    after = {order[i]: order[(i + 1) % n] for i in range(n)}
    ring = [(2 * i + k, 2 * after[i] + k) for i in range(n) for k in range(2)]
    back = [(j, i) for i, j in ring]
    twin = [(i, i ^ 1) for i in range(2 * n)]
    began = [look_up(order, (look_up(place, q) - t) % n) for t in range(n)]
    scalars = jnp.stack([core, *began]).astype(jnp.int32)

    def peers(d):
        return [(i, i ^ d) for i in range(n)]

    width = transform.shape[1]
    rows = jnp.concatenate([b_gate_up, b_down], axis=0)
    part_rows = 2 * rows.shape[0] // n

    def cat(arrays):
        return arrays[0] if len(arrays) == 1 else jnp.concatenate(arrays, axis=0)

    def along_ring(perm, name, held, step):
        if not step:
            return None
        with jax.named_scope(name):
            return lax.ppermute(cat([held[t][i] for t, i, _ in step]), "col", perm)

    def split(arrived, held, step):
        for i, (t, _, to) in enumerate(step):
            held[t][to] = arrived[i * part_rows : (i + 1) * part_rows]

    def for_row(held, r):
        return pick([held[i] for i in range(n)], (look_up(place, r) - look_up(place, z)) % n)

    half = n // 2
    partial, sums, held, got = {}, {}, {}, {}
    sofar, ready = [], None
    for step in range(n + half + 3):
        out = {}
        if step < n:
            if step < n - 1:
                with jax.named_scope(f"rows_ring_{step}"):
                    out["rows"] = lax.ppermute(rows, "col", ring)
            with jax.named_scope(f"rows_twin_{step}"):
                other = lax.ppermute(rows, "col", twin)
            out["partial"] = project(scalars, rows, other, transform)
        if 0 <= step - 1 < n:
            parts = partial[step - 1].reshape(n, part_rows, width)
            out["sums"] = [lax.dynamic_index_in_dim(parts, q, keepdims=False)]
            for d in range(1, n):
                with jax.named_scope(f"reduce_{step - 1}_{d}"):
                    part = lax.dynamic_index_in_dim(parts, q ^ d, keepdims=False)
                    out["sums"].append(lax.ppermute(part, "row", peers(d)))
        if 0 <= step - 2 < n:
            held[step - 2] = {0: sum(v.astype(F32) for v in sums[step - 2]).astype(BF16)}
        onward, backward = [], []
        for t in range(n):
            hop = step - 2 - t
            if 0 <= hop < half:
                onward.append((t, hop, hop + 1))
                if t == n - 1:
                    if hop + 1 < half:
                        backward.append((t, -hop % n, n - hop - 1))
                elif hop:
                    backward.append((t, (1 - hop) % n, n - hop))
        out["onward"] = along_ring(back, f"shares_onward_{step}", held, onward)
        out["backward"] = along_ring(ring, f"shares_backward_{step}", held, backward)
        deliver = [t for t in range(n) if step == max(t + 2 + half, n + 1)]
        if deliver:
            out["got"] = [cat([for_row(held[t], q) for t in deliver])]
            for d in range(1, n):
                with jax.named_scope(f"deliver_{step}_{d}"):
                    out["got"].append(lax.ppermute(cat([for_row(held[t], q ^ d) for t in deliver]), "row", peers(d)))
        if got:
            arrived = got.pop(step - 1)
            count = arrived[0].shape[0] // part_rows
            pieces = []
            for i in range(count):
                own = [v[i * part_rows : (i + 1) * part_rows] for v in arrived]
                pieces += [pick(own, q ^ j) for j in range(n)]
            own = cat(pieces)
            with jax.named_scope(f"deliver_twin_{step}"):
                far = lax.ppermute(own, "col", twin)
            for i, t in enumerate(delivered):
                if t < n - 1:
                    sofar = merge_group(scalars, t, n, i, own, far, a_gate_up, a_down, sofar)
            if n - 1 not in delivered:
                ready = ready_half(scalars, check_tokens, n - 1, n, sofar[0]) if n - 2 in delivered else None
        out["sofar"] = sofar
        out["ready"] = ready

        leaves, tree = jax.tree.flatten(out)
        out = jax.tree.unflatten(tree, lax.optimization_barrier(leaves))
        rows = out.get("rows")
        if "partial" in out:
            partial[step] = out["partial"]
        if "sums" in out:
            sums[step - 1] = out["sums"]
        split(out["onward"], held, onward)
        split(out["backward"], held, backward)
        if "got" in out:
            got[step] = out["got"]
            delivered = deliver
        sofar, ready = out["sofar"], out["ready"]

    merged_gate_up, merged_down, parts = forward(
        scalars, check_tokens, n - 1, n, own, far, a_gate_up, a_down, ready, sofar
    )
    total = lax.dynamic_index_in_dim(parts, q, keepdims=False).astype(F32)
    for d in range(1, n):
        with jax.named_scope(f"check_reduce_{d}"):
            sent = lax.dynamic_index_in_dim(parts, q ^ d, keepdims=False)
            total = total + lax.ppermute(sent, "row", peers(d)).astype(F32)
    hidden_units = n * transform.shape[0]
    check = (total * hidden_units ** (-0.5)).astype(BF16)
    count, features = check_tokens.shape
    share = features // n
    check = check.reshape(check.shape[0], -1, share).swapaxes(0, 1).reshape(count, share)
    return merged_gate_up, merged_down, check


def solution(mesh):
    return jax.shard_map(
        on_device,
        mesh=mesh,
        in_specs=(
            P("col", "row"),
            P("col", "row"),
            P(None, "row"),
            P(None, "row"),
            P("row", "col"),
            P("col", None),
        ),
        out_specs=(P(None, "row"), P(None, "row"), P("col", "row")),
        check_vma=False,
    )
```
